32 devices in a mesh: space: 8 (over z, x), kern: 4 (over y, core).
Axes of the slice: x: 2, y: 2, z: 4, core: 2. Of those that a mesh axis runs over, the one named last changes fastest.
Arguments:
- mask: bfloat16 [4096, 4096], P('space'), may hold values from -1 to 1
- kernels: float32 [2, 16, 512, 512], P(None, 'kern', 'space'), may hold values from -4 to 4
- target: int32 [1024, 1024], P('space'), may hold values 0 or 1
Outputs:
- gradient: float32 [4096, 4096], P('space')
- resist: float32 [1024, 1024], P('space')
The draws below stay inside these ranges and needn't reach their ends.
All inputs are finite; a program needn't handle non-finite values. No bound on the sum of `target` on one device may be relied on, other than what follows from the above.
Results may differ from the reference program's by a relative error of at most 0.0003.
Values sent between devices are 32-bit elements; how exact they have to be, the bound alone decides.
A program may use at most 64 MiB of HBM per device.

```python
import jax
import jax.numpy as jnp
from jax import lax

N = 4096
B = 512
G = 1024
K = 16


def plant(result, key, least, top_value):
    spot = [jax.random.randint(jax.random.fold_in(key, axis), (), 0, length) for axis, length in enumerate(result.shape)]
    longest = result.shape.index(max(result.shape))
    beside = spot[:longest] + [(spot[longest] + 1) % result.shape[longest]] + spot[longest + 1:]
    return result.at[tuple(spot)].set(least).at[tuple(beside)].set(top_value)


def levels(stream_key, extent, pieces, smallest, high):
    loudness, own = 1.0, jax.random.fold_in(stream_key, 6)
    for dim, shards_of in pieces:
        draws = jnp.exp(jax.random.uniform(jax.random.fold_in(own, dim), (shards_of,), jnp.float32, smallest / len(pieces), high / len(pieces)))
        loudness = loudness * jnp.repeat(draws, extent[dim] // shards_of).reshape([-1 if axis == dim else 1 for axis in range(len(extent))])
    return loudness


def scatter_about(stream_key, extent, scale, most, pieces=(), kind=jnp.bfloat16):
    loudness = levels(stream_key, extent, pieces, -0.22, 0.18) if pieces else 1.0
    result = jax.random.normal(stream_key, extent, jnp.float32) * scale * loudness
    return jnp.minimum(jnp.maximum(result, -most), most).astype(kind)


def setup_inputs(seed: int = 0) -> dict:
    keys = jax.random.split(jax.random.key(seed), 4)
    return {
        "mask": jnp.clip(jax.random.uniform(keys[0], (N, N), jnp.float32, -1.0, 1.0) * levels(keys[0], (N, N), ((0, 8),), -0.4, 0.0), -1.0, 1.0).astype(jnp.bfloat16),
        "kernels": scatter_about(keys[1], (2, K, B, B), 0.3, 4.0, ((1, 4), (2, 8)), jnp.float32),
        "target": plant((jax.random.randint(keys[2], (G, G), 0, 2) < 1).astype(jnp.int32), jax.random.fold_in(keys[2], 1), 0, 1),
    }


steepness = 8.0
threshold = 1.5
highest = lax.Precision.HIGHEST


def phases(left, right, modulus):
    product = (left[:, None] * right[None, :]) % modulus
    return product.astype(jnp.float32) * (2.0 * jnp.pi / modulus)


def column_table(pixels, frequency, length):
    angle = phases(pixels, frequency, length)
    return jnp.concatenate([jnp.cos(angle), -jnp.sin(angle)], axis=1)


def row_table(pixels, frequency, length):
    angle = phases(pixels, frequency, length)
    return jnp.concatenate([jnp.cos(angle), -jnp.sin(angle)], axis=1) / length


def grid_table(frequency, points):
    angle = phases(frequency, jnp.arange(points, dtype=jnp.int32), points)
    return jnp.concatenate([jnp.cos(angle), jnp.sin(angle)], axis=1)


def reference(mask, kernels, target):
    frequency = jnp.arange(B, dtype=jnp.int32) - B // 2
    pixels = jnp.arange(N, dtype=jnp.int32)
    col_tab = column_table(pixels, frequency, N)
    row_tab = row_table(pixels, frequency, N)
    grid = grid_table(frequency, G)
    columns = lax.dot_general(col_tab, mask.astype(jnp.float32), (((0,), (1,)), ((), ())), precision=highest)
    total = jnp.dot(columns, row_tab, precision=highest)
    spec_re = total[:B, :B] - total[B:, B:]
    spec_im = total[:B, B:] + total[B:, :B]
    kern_re = kernels[0]
    kern_im = kernels[1]
    prod_re = kern_re * spec_re - kern_im * spec_im
    prod_im = kern_re * spec_im + kern_im * spec_re
    lifted = jnp.dot(jnp.stack([prod_re, prod_im]).reshape(2 * K * B, B), grid, precision=highest).reshape(2, K, B, 2 * G)
    coarse_re = lifted[0, :, :, :G] - lifted[1, :, :, G:]
    coarse_im = lifted[0, :, :, G:] + lifted[1, :, :, :G]
    image = lax.dot_general(jnp.stack([coarse_re, coarse_im]), grid, (((2,), (0,)), ((), ())), precision=highest)
    field_re = image[0, :, :, :G] - image[1, :, :, G:]
    field_im = image[0, :, :, G:] + image[1, :, :, :G]
    intensity = jnp.sum(field_re * field_re + field_im * field_im, axis=0) / (B * B)
    resist = jax.nn.sigmoid(steepness * (intensity - threshold))
    slope = 2.0 * (resist - target.astype(jnp.float32)) * steepness * resist * (1.0 - resist)
    scale = 2.0 * slope / (B * B)
    grad_re = scale * field_re
    grad_im = scale * field_im
    mixed = jnp.stack([jnp.concatenate([grad_re, grad_im], axis=-1), jnp.concatenate([grad_im, -grad_re], axis=-1)])
    back = lax.dot_general(grid, mixed, (((1,), (3,)), ((), ())), precision=highest)
    back_re = back[:, 0]
    back_im = back[:, 1]
    mixed_two = jnp.stack([jnp.concatenate([back_re, back_im], axis=-1), jnp.concatenate([back_im, -back_re], axis=-1)])
    spectral = lax.dot_general(mixed_two, grid, (((3,), (1,)), ((), ())), precision=highest)
    kern_swap = jnp.swapaxes(kernels, 1, 2)
    sum_re = jnp.sum(kern_swap[0] * spectral[0] + kern_swap[1] * spectral[1], axis=1)
    sum_im = jnp.sum(kern_swap[0] * spectral[1] - kern_swap[1] * spectral[0], axis=1)
    stacked = jnp.concatenate([jnp.concatenate([sum_re, sum_im], axis=1), jnp.concatenate([sum_im, -sum_re], axis=1)], axis=0)
    delta = lax.dot_general(stacked, row_tab, (((1,), (1,)), ((), ())), precision=highest)
    gradient = lax.dot_general(delta, col_tab, (((0,), (1,)), ((), ())), precision=highest)
    return gradient, resist
```

```python
import functools

import jax
import jax.numpy as jnp
import ml_dtypes
import numpy as np
from jax import lax
from jax.experimental import pallas as pl
from jax.experimental.pallas import tpu as pltpu
from jax.sharding import PartitionSpec as P

N = 4096
B = 512
G = 1024


steepness = 8.0
threshold = 1.5
highest = lax.Precision.HIGHEST
block_limit = 1024


def phases(left, right, modulus):
    product = left[:, None] * right[None, :] % modulus
    return product.astype(jnp.float32) * (2.0 * jnp.pi / modulus)


def column_table(pixels, frequency, length):
    angle = phases(pixels, frequency, length)
    return jnp.concatenate([jnp.cos(angle), -jnp.sin(angle)], axis=1)


def row_table(pixels, frequency, length):
    angle = phases(pixels, frequency, length)
    return jnp.concatenate([jnp.cos(angle), -jnp.sin(angle)], axis=1) / length


def grid_table(frequency, points):
    angle = phases(frequency, jnp.arange(points, dtype=jnp.int32), points)
    return jnp.concatenate([jnp.cos(angle), jnp.sin(angle)], axis=1)


def forward_columns(mask, frequency):
    rows = mask.shape[0]
    span = min(block_limit, N)
    count = frequency.shape[0]

    def step(index, running):
        start = index * span
        table = column_table(start + jnp.arange(span, dtype=jnp.int32), frequency, N)
        piece = lax.dynamic_slice_in_dim(mask, start, span, 1).astype(jnp.float32)
        return running + lax.dot_general(table, piece, (((0,), (1,)), ((), ())), precision=highest)

    running = lax.fori_loop(0, N // span, step, jnp.zeros((2 * count, rows), jnp.float32))
    return running.reshape(2, count, rows)


def forward_rows(arrived):
    count = arrived.shape[1]
    flat = arrived.reshape(2 * count, N)
    frequency = jnp.arange(B, dtype=jnp.int32) - B // 2
    span = min(block_limit, N)

    def step(index, running):
        start = index * span
        table = row_table(start + jnp.arange(span, dtype=jnp.int32), frequency, N)
        piece = lax.dynamic_slice_in_dim(flat, start, span, 1)
        return running + jnp.dot(piece, table, precision=highest)

    running = lax.fori_loop(0, N // span, step, jnp.zeros((2 * count, 2 * B), jnp.float32))
    real_part = running[:count, :B] - running[count:, B:]
    imag_part = running[:count, B:] + running[count:, :B]
    return jnp.stack([real_part, imag_part])


def adjoint_rows(sum_re, sum_im):
    count = sum_re.shape[0]
    stacked = jnp.concatenate(
        [jnp.concatenate([sum_re, sum_im], axis=1), jnp.concatenate([sum_im, -sum_re], axis=1)],
        axis=0,
    )
    frequency = jnp.arange(B, dtype=jnp.int32) - B // 2
    span = min(block_limit, N)

    def step(index, output):
        start = index * span
        table = row_table(start + jnp.arange(span, dtype=jnp.int32), frequency, N)
        piece = lax.dot_general(stacked, table, (((1,), (1,)), ((), ())), precision=highest)
        return lax.dynamic_update_slice_in_dim(output, piece, start, 1)

    output = lax.fori_loop(0, N // span, step, jnp.zeros((2 * count, N), jnp.float32))
    return output.reshape(2, count, N)


def add_columns(total, spectrum, frequency):
    span = min(block_limit, N)

    def step(index, running):
        start = index * span
        table = column_table(start + jnp.arange(span, dtype=jnp.int32), frequency, N)
        piece = lax.dot_general(spectrum, table, (((0,), (1,)), ((), ())), precision=highest)
        current = lax.dynamic_slice_in_dim(running, start, span, 1)
        return lax.dynamic_update_slice_in_dim(running, current + piece, start, 1)

    return lax.fori_loop(0, N // span, step, total)


def local(mask, kernels, target):
    rows = mask.shape[0]
    kern_count = lax.axis_size("kern")
    space_count = lax.axis_size("space")
    group = lax.axis_index("kern")
    per_space = B // space_count
    per_group = per_space // kern_count
    frequency = jnp.arange(B, dtype=jnp.int32) - B // 2
    subset = (
        per_space * jnp.arange(space_count, dtype=jnp.int32)[:, None]
        + per_group * group
        + jnp.arange(per_group, dtype=jnp.int32)[None, :]
    )
    columns = forward_columns(mask, subset.reshape(-1) - B // 2)
    arrived = lax.all_to_all(columns, "space", split_axis=1, concat_axis=2, tiled=True)
    spectrum = lax.all_gather(forward_rows(arrived), "kern", axis=1, tiled=True)
    kern_swap = jnp.swapaxes(kernels, 1, 2)
    kernel_count = kern_swap.shape[2]
    spec_re = spectrum[0][:, None, :]
    spec_im = spectrum[1][:, None, :]
    prod_re = kern_swap[0] * spec_re - kern_swap[1] * spec_im
    prod_im = kern_swap[0] * spec_im + kern_swap[1] * spec_re
    grid = grid_table(frequency, G)
    lifted = jnp.dot(
        jnp.stack([prod_re, prod_im]).reshape(2 * per_space * kernel_count, B),
        grid,
        precision=highest,
    )
    lifted = lifted.reshape(2, per_space, kernel_count, 2 * G)
    coarse_re = lifted[0, :, :, :G] - lifted[1, :, :, G:]
    coarse_im = lifted[0, :, :, G:] + lifted[1, :, :, :G]
    coarse = jnp.stack([coarse_re, coarse_im], axis=1)
    gathered = lax.all_to_all(coarse, "space", split_axis=3, concat_axis=0, tiled=True)
    grid_rows = gathered.shape[3]
    image = lax.dot_general(
        gathered.reshape(B, 2 * kernel_count * grid_rows),
        grid,
        (((0,), (0,)), ((), ())),
        precision=highest,
    )
    image = image.reshape(2, kernel_count, grid_rows, 2 * G)
    field_re = image[0, :, :, :G] - image[1, :, :, G:]
    field_im = image[0, :, :, G:] + image[1, :, :, :G]
    partial_light = jnp.sum(field_re * field_re + field_im * field_im, axis=0) / (B * B)
    intensity = lax.psum(partial_light, "kern")
    resist = jax.nn.sigmoid(steepness * (intensity - threshold))
    slope = 2.0 * (resist - target.astype(jnp.float32)) * steepness * resist * (1.0 - resist)
    scale = 2.0 * slope / (B * B)
    grad_re = scale * field_re
    grad_im = scale * field_im
    mixed = jnp.stack(
        [
            jnp.concatenate([grad_re, grad_im], axis=-1),
            jnp.concatenate([grad_im, -grad_re], axis=-1),
        ]
    )
    mixed = mixed.reshape(2 * kernel_count * grid_rows, 2 * G)
    backward = lax.dot_general(grid, mixed, (((1,), (1,)), ((), ())), precision=highest)
    backward = backward.reshape(B, 2, kernel_count, grid_rows)
    returned = lax.all_to_all(backward, "space", split_axis=0, concat_axis=3, tiled=True)
    back_re = returned[:, 0]
    back_im = returned[:, 1]
    mixed_two = jnp.stack(
        [
            jnp.concatenate([back_re, back_im], axis=-1),
            jnp.concatenate([back_im, -back_re], axis=-1),
        ]
    )
    mixed_two = mixed_two.reshape(2 * per_space * kernel_count, 2 * G)
    spectral = lax.dot_general(mixed_two, grid, (((1,), (1,)), ((), ())), precision=highest)
    spectral = spectral.reshape(2, per_space, kernel_count, B)
    sum_re = jnp.sum(kern_swap[0] * spectral[0] + kern_swap[1] * spectral[1], axis=1)
    sum_im = jnp.sum(kern_swap[0] * spectral[1] - kern_swap[1] * spectral[0], axis=1)
    empty = jnp.zeros((rows, N), jnp.float32)
    shares = (
        lax.psum_scatter(sum_re, "kern", scatter_dimension=0, tiled=True),
        lax.psum_scatter(sum_im, "kern", scatter_dimension=0, tiled=True),
    )
    delta = adjoint_rows(shares[0], shares[1])
    landed = lax.all_to_all(delta, "space", split_axis=2, concat_axis=1, tiled=True)
    ordering = (
        per_group * jnp.arange(kern_count, dtype=jnp.int32)[:, None, None]
        + per_space * jnp.arange(space_count, dtype=jnp.int32)[None, :, None]
        + jnp.arange(per_group, dtype=jnp.int32)[None, None, :]
    )
    ordered_freq = ordering.reshape(-1) - B // 2
    piece = lax.all_gather(landed, "kern", axis=1, tiled=True)
    width = piece.shape[1]
    gradient = add_columns(empty, piece.reshape(2 * width, rows), ordered_freq)
    return (gradient, resist)


MESH = pl.DeviceIdType.MESH


def split_constant(values):
    high = values.astype(np.float32).astype(ml_dtypes.bfloat16)
    low = (values - high.astype(np.float64)).astype(ml_dtypes.bfloat16)
    return jnp.asarray(high), jnp.asarray(low)


def pixel_table(S, Q):
    nx, P_ = S // Q, B // S
    g = P_ // Q
    y, z, x, i = np.meshgrid(np.arange(Q), np.arange(Q), np.arange(nx), np.arange(g), indexing="ij")
    f = ((y * nx + x) * P_ + z * g + i - B // 2).reshape(-1, g)
    angle = (f[:, :, None] * np.arange(N)) % N * (2 * np.pi / N)
    table = np.stack([np.cos(angle), -np.sin(angle)], axis=1)
    return jnp.asarray(table.reshape(2 * B, N).astype(np.float32))


def coarse_tables(S):
    f = np.arange(B) - B // 2
    points = np.arange(G)
    angle = (f[:, None] * points[None, :]) % G * (2 * np.pi / G)
    c, s = np.cos(angle), np.sin(angle)
    Y = G // S
    cc = c.reshape(B, S, Y).transpose(1, 0, 2)
    ss = s.reshape(B, S, Y).transpose(1, 0, 2)
    lift = np.concatenate([np.concatenate([cc, ss], 2), np.concatenate([-ss, cc], 2)], 1)
    forward = np.concatenate([c.T, s.T], 0)
    backward = np.concatenate([c, s], 0)
    return split_constant(lift) + split_constant(forward) + split_constant(backward)


def halves(value):
    high = value.astype(jnp.bfloat16)
    return high, (value - high.astype(jnp.float32)).astype(jnp.bfloat16)


def dot3(ah, al, bh, bl, dims):
    d = functools.partial(lax.dot_general, dimension_numbers=(dims, ((), ())), preferred_element_type=jnp.float32)
    return d(ah, bh) + (d(al, bh) + d(ah, bl))


NN = ((1,), (0,))
NT = ((1,), (1,))


def remote(src, dst, send, recv, space, kern):
    return pltpu.make_async_remote_copy(
        src_ref=src, dst_ref=dst, send_sem=send, recv_sem=recv, device_id=(space, kern), device_id_type=MESH
    )


def scatter_kernel(S, R, x_ref, out_ref, send, recv, own):
    sp, kq = lax.axis_index("space"), lax.axis_index("kern")
    barrier = pltpu.get_barrier_semaphore()

    def greet(o, c):
        pl.semaphore_signal(barrier, inc=1, device_id=(lax.rem(sp + o, S), kq), device_id_type=MESH)
        return c

    lax.fori_loop(1, S, greet, 0)
    pl.semaphore_wait(barrier, S - 1)
    place = lambda s: out_ref.at[:, pl.ds(pl.multiple_of(s * R, R), R)]
    local_copy = pltpu.make_async_copy(x_ref.at[sp], place(sp), own)
    local_copy.start()

    def launch(o, c):
        d = lax.rem(sp + o, S)
        remote(x_ref.at[d], place(sp), send.at[d], recv.at[sp], d, kq).start()
        return c

    lax.fori_loop(1, S, launch, 0)

    def finish(o, c):
        d = lax.rem(sp + o, S)
        remote(x_ref.at[d], place(d), send.at[d], recv.at[d], d, kq).wait()
        return c

    lax.fori_loop(1, S, finish, 0)
    local_copy.wait()


def gather_kernel(S, Q, R, x_ref, out_ref, send, recv, ysend, yrecv, csend, crecv, own):
    sp, kq = lax.axis_index("space"), lax.axis_index("kern")
    kc = kq + 1 - 2 * lax.rem(kq, 2)
    ky = lax.rem(kq + 2, Q)
    kyc = lax.rem(kc + 2, Q)
    barrier = pltpu.get_barrier_semaphore()

    def greet(o, c):
        pl.semaphore_signal(barrier, inc=1, device_id=(lax.rem(sp + o, S), kq), device_id_type=MESH)
        return c

    lax.fori_loop(1, S, greet, 0)
    for k in (kc, ky):
        pl.semaphore_signal(barrier, inc=1, device_id=(sp, k), device_id_type=MESH)
    pl.semaphore_wait(barrier, S + 1)
    slab = lambda s: x_ref.at[:, pl.ds(pl.multiple_of(s * R, R), R)]

    def launch(o, c):
        d = lax.rem(sp + o, S)
        remote(slab(d), out_ref.at[kq, sp], send.at[d], recv.at[sp], d, kq).start()
        return c

    lax.fori_loop(1, S, launch, 0)
    local_copy = pltpu.make_async_copy(slab(sp), out_ref.at[kq, sp], own)
    local_copy.start()
    local_copy.wait()

    def to_y(s, group):
        return remote(out_ref.at[group, s], out_ref.at[group, s], ysend.at[s], yrecv.at[s], sp, ky)

    def to_core(s, group, slot):
        return remote(out_ref.at[group, s], out_ref.at[group, s], csend.at[slot, s], crecv.at[slot, s], sp, kc)

    to_y(sp, kq).start()
    to_core(sp, kq, 0).start()

    def onward(o, c):
        s = lax.rem(sp + S - o, S)
        remote(slab(s), out_ref.at[kq, s], send.at[s], recv.at[s], s, kq).wait_recv()
        to_y(s, kq).start()
        to_core(s, kq, 0).start()
        return c

    lax.fori_loop(1, S, onward, 0)

    def across(o, c):
        s = lax.rem(sp + S - o, S)
        to_y(s, ky).wait_recv()
        to_core(s, ky, 1).start()
        return c

    lax.fori_loop(0, S, across, 0)

    def finish(s, c):
        to_y(s, kq).wait_send()
        to_core(s, kq, 0).wait_send()
        to_core(s, ky, 1).wait_send()
        to_core(s, kc, 0).wait_recv()
        to_core(s, kyc, 1).wait_recv()
        return c

    lax.fori_loop(0, S, finish, 0)

    def sent(o, c):
        d = lax.rem(sp + o, S)
        remote(slab(d), out_ref.at[kq, sp], send.at[d], recv.at[sp], d, kq).wait_send()
        return c

    lax.fori_loop(1, S, sent, 0)


def imaging_kernel(
    S, Q, K4,
    spec_ref, kern_ref, target_ref, lh_hbm, ll_hbm, fh_hbm, fl_hbm, bh_hbm, bl_hbm,
    out_ref, resist_ref,
    lh, ll, fh, fl, bh, bl, table_sem,
    specall, ph, pw, out1, in1, field, light, lightin, lightall, out2, in2, sums, rsin, acc,
    spec_s, spec_r, s1, r1, ls, lr, as_, ar, s2, r2, rs, rr,
):
    nx, P_, Y = S // Q, B // S, G // S
    g = P_ // Q
    GQ = G // Q
    sp, kq = lax.axis_index("space"), lax.axis_index("kern")
    z, x = sp // nx, lax.rem(sp, nx)
    blk = kq * nx + x
    tables = [
        pltpu.make_async_copy(src, dst, table_sem.at[i])
        for i, (src, dst) in enumerate(
            zip((lh_hbm, ll_hbm, fh_hbm, fl_hbm, bh_hbm, bl_hbm), (lh, ll, fh, fl, bh, bl))
        )
    ]
    for t in tables:
        t.start()

    def member(o):
        b = lax.rem(blk + o, S)
        return b, z * nx + lax.rem(b, nx), b // nx

    def zpeer(o):
        q = lax.rem(z + o, Q)
        return q, q * nx + x

    barrier = pltpu.get_barrier_semaphore()

    def greet(o, c):
        b, s, k = member(o)
        pl.semaphore_signal(barrier, inc=1, device_id=(s, k), device_id_type=MESH)
        return c

    lax.fori_loop(1, S, greet, 0)
    for o in range(1, Q):
        pl.semaphore_signal(barrier, inc=1, device_id=(zpeer(o)[1], kq), device_id_type=MESH)
    pl.semaphore_wait(barrier, S + Q - 2)

    def spec_copy(o, slot):
        q, s = zpeer(o)
        return remote(spec_ref, specall.at[slot], spec_s.at[q], spec_r.at[slot], s, kq)

    for o in range(1, Q):
        spec_copy(o, z).start()
    specall[z] = spec_ref[...]
    for o in range(1, Q):
        spec_copy(o, zpeer(o)[0]).wait()

    spec = specall[...].reshape(P_, 2 * B)
    sr, si = spec[:, :B], spec[:, B:]
    for k in range(K4):
        kr, ki = kern_ref[0, k], kern_ref[1, k]
        rows = pl.ds(k * P_, P_)
        ph[rows, :B], pw[rows, :B] = halves(kr * sr - ki * si)
        ph[rows, B:], pw[rows, B:] = halves(kr * si + ki * sr)

    tables[0].wait()
    tables[1].wait()
    pair = K4 // 2

    def copy1(k, b, s, kk, slot):
        return remote(out1.at[k, b], in1.at[k, slot], s1.at[k, b], r1.at[k, slot], s, kk)

    for h in range(2):
        rows = pl.ds(h * pair * P_, pair * P_)
        own = None

        def lift(b):
            return dot3(ph[rows, :], pw[rows, :], lh[b], ll[b], NN).reshape(pair, P_, 2 * Y)

        def step(o, c):
            b, s, kk = member(o)
            value = lift(b)
            for j in range(pair):
                out1[h * pair + j, b] = value[j]
            for j in range(pair):
                copy1(h * pair + j, b, s, kk, blk).start()
            return c

        lax.fori_loop(1, S, step, 0)
        value = lift(blk)
        for j in range(pair):
            in1[h * pair + j, blk] = value[j]

    for t in tables[2:]:
        t.wait()
    chunk = 256

    def image(k, c):
        def arrive(o, c):
            b, s, kk = member(o)
            copy1(k, b, s, kk, b).wait_recv()
            return c

        lax.fori_loop(1, S, arrive, 0)
        dh, dl = halves(in1[k].reshape(B, 2 * Y))

        def part(j, c):
            rows = pl.ds(pl.multiple_of(j * chunk, chunk), chunk)
            low = pl.ds(pl.multiple_of(G + j * chunk, chunk), chunk)
            a = dot3(fh[rows, :], fl[rows, :], dh, dl, NN)
            b = dot3(fh[low, :], fl[low, :], dh, dl, NN)
            re = a[:, :Y] - b[:, Y:]
            im = a[:, Y:] + b[:, :Y]
            field[k, rows, :Y] = re
            field[k, rows, Y:] = im
            power = re * re + im * im

            @pl.when(k == 0)
            def _():
                light[rows, :] = power

            @pl.when(k > 0)
            def _():
                light[rows, :] = light[rows, :] + power

            return c

        return lax.fori_loop(0, G // chunk, part, c)

    lax.fori_loop(0, K4, image, 0)

    quarter = lambda q: pl.ds(pl.multiple_of(q * GQ, GQ), GQ)

    def light_copy(o, slot):
        q, s = zpeer(o)
        return remote(light.at[quarter(q)], lightin.at[slot], ls.at[q], lr.at[slot], s, kq)

    for o in range(1, Q):
        light_copy(o, z).start()
    lightin[z] = light[quarter(z), :]
    for o in range(1, Q):
        light_copy(o, zpeer(o)[0]).wait()
    total = lightin[0]
    for q in range(1, Q):
        total = total + lightin[q]
    lightall[z] = total * (1.0 / (B * B))

    def all_copy(o, slot):
        q, s = zpeer(o)
        return remote(lightall.at[z], lightall.at[slot], as_.at[q], ar.at[slot], s, kq)

    for o in range(1, Q):
        all_copy(o, z).start()
    for o in range(1, Q):
        all_copy(o, zpeer(o)[0]).wait_recv()
    for q in range(Q):
        rows = pl.ds(q * GQ, GQ)
        resist = jax.nn.sigmoid(steepness * (lightall[q] - threshold))
        resist_ref[rows, :] = resist
        light[rows, :] = (4.0 * steepness / (B * B)) * (resist - target_ref[rows, :]) * resist * (1.0 - resist)

    def copy2(k, b, s, kk, slot):
        return remote(out2.at[k, b], in2.at[k, slot], s2.at[k, b], r2.at[k, slot], s, kk)

    def back(k, c):
        scale = light[...]
        scale = jnp.concatenate([scale, scale], axis=1)
        dh, dl = halves(field[k] * scale)

        def part(j, c):
            rows = pl.ds(pl.multiple_of(j * chunk, chunk), chunk)
            low = pl.ds(pl.multiple_of(B + j * chunk, chunk), chunk)
            a = dot3(bh[rows, :], bl[rows, :], dh, dl, NN)
            b = dot3(bh[low, :], bl[low, :], dh, dl, NN)
            value = jnp.concatenate([a[:, :Y] + b[:, Y:], a[:, Y:] - b[:, :Y]], axis=1)
            out2[k, pl.ds(j * (chunk // P_), chunk // P_)] = value.reshape(chunk // P_, P_, 2 * Y)
            return c

        lax.fori_loop(0, B // chunk, part, c)

        def launch(o, c):
            b, s, kk = member(o)
            copy2(k, b, s, kk, blk).start()
            return c

        lax.fori_loop(1, S, launch, 0)
        in2[k, blk] = out2[k, blk]
        return c

    lax.fori_loop(0, K4, back, 0)

    sum_re = jnp.zeros((P_, B), jnp.float32)
    sum_im = jnp.zeros((P_, B), jnp.float32)
    for h in range(2):
        for j in range(pair):
            def arrive2(o, c):
                b, s, kk = member(o)
                copy2(h * pair + j, b, s, kk, b).wait_recv()
                return c

            lax.fori_loop(1, S, arrive2, 0)
        acc[...] = jnp.zeros_like(acc)

        def add(s, c):
            dh, dl = halves(in2[pl.ds(h * pair, pair), s].reshape(pair * P_, 2 * Y))
            acc[...] += dot3(dh, dl, lh[s], ll[s], NT)
            return c

        lax.fori_loop(0, S, add, 0)
        for j in range(pair):
            k = h * pair + j
            kr, ki = kern_ref[0, k], kern_ref[1, k]
            pr, pi = acc[pl.ds(j * P_, P_), :B], acc[pl.ds(j * P_, P_), B:]
            sum_re = sum_re + kr * pr + ki * pi
            sum_im = sum_im + kr * pi - ki * pr
    sums[:, :, :B] = sum_re.reshape(Q, g, B)
    sums[:, :, B:] = sum_im.reshape(Q, g, B)

    def sum_copy(o, slot):
        q, s = zpeer(o)
        return remote(sums.at[q], rsin.at[slot], rs.at[q], rr.at[slot], s, kq)

    for o in range(1, Q):
        sum_copy(o, z).start()
    rsin[z] = sums[z]
    for o in range(1, Q):
        sum_copy(o, zpeer(o)[0]).wait()
    total = rsin[0]
    for q in range(1, Q):
        total = total + rsin[q]
    out_ref[...] = total

    for o in range(1, Q):
        all_copy(o, z).wait_send()

    def drain(k, c):
        def one(o, c):
            b, s, kk = member(o)
            copy1(k, b, s, kk, blk).wait_send()
            copy2(k, b, s, kk, blk).wait_send()
            return c

        return lax.fori_loop(1, S, one, c)

    lax.fori_loop(0, K4, drain, 0)


def call(kernel, outs, specs, scratch, cid, args, mib):
    vm = pl.BlockSpec(memory_space=pltpu.VMEM)
    return pl.pallas_call(
        kernel,
        out_shape=outs,
        in_specs=specs,
        out_specs=jax.tree.map(lambda _: vm, outs),
        scratch_shapes=scratch,
        compiler_params=pltpu.CompilerParams(
            collective_id=cid, has_side_effects=True, vmem_limit_bytes=mib * 2**20
        ),
    )(*args)


def fast(S, Q, mask, kernels, target):
    f32, bf16 = jnp.float32, jnp.bfloat16
    nx, P_, Y, R = S // Q, B // S, G // S, N // S
    g, K4 = P_ // Q, kernels.shape[1]
    DMA = pltpu.SemaphoreType.DMA
    vm, any_ = pl.BlockSpec(memory_space=pltpu.VMEM), pl.BlockSpec(memory_space=pl.ANY)
    high = lax.Precision.HIGH
    kq = lax.axis_index("kern")
    table = pixel_table(S, Q)
    swap = [
        (((zz * nx) + xx) * Q + kk, ((kk * nx) + xx) * Q + zz)
        for zz in range(Q) for xx in range(nx) for kk in range(Q)
    ]
    kern_here = lax.ppermute(kernels, ("space", "kern"), swap)
    target_here = lax.ppermute(target, ("space", "kern"), swap).T.astype(f32)

    rows = lax.dynamic_slice_in_dim(table, kq * (2 * B // Q), 2 * B // Q, 0)
    columns = lax.dot_general(rows, mask.astype(f32), (((1,), (1,)), ((), ())), precision=high)
    arrived = call(
        functools.partial(scatter_kernel, S, R),
        jax.ShapeDtypeStruct((2 * g, N), f32), [vm],
        [DMA((S,)), DMA((S,)), DMA],
        0, (columns.reshape(S, 2 * g, R),), 16,
    )
    t = lax.dot_general(arrived, table, (((1,), (1,)), ((), ())), precision=high) * (1.0 / N)
    t = t.reshape(2, g, Q, Q, nx, 2, g).transpose(0, 1, 5, 2, 4, 3, 6).reshape(2, g, 2, B)
    spec = jnp.concatenate([t[0, :, 0] - t[1, :, 1], t[0, :, 1] + t[1, :, 0]], axis=1)

    consts = coarse_tables(S)
    V = pltpu.VMEM
    total, resist = call(
        functools.partial(imaging_kernel, S, Q, K4),
        (jax.ShapeDtypeStruct((g, 2 * B), f32), jax.ShapeDtypeStruct((G, Y), f32)),
        [vm, vm, vm] + [any_] * 6,
        [V(c.shape, bf16) for c in consts] + [DMA((6,))] + [
            V((Q, g, 2 * B), f32),
            V((K4 * P_, 2 * B), bf16), V((K4 * P_, 2 * B), bf16),
            V((K4, S, P_, 2 * Y), f32), V((K4, S, P_, 2 * Y), f32),
            V((K4, G, 2 * Y), f32), V((G, Y), f32),
            V((Q, G // Q, Y), f32), V((Q, G // Q, Y), f32),
            V((K4, S, P_, 2 * Y), f32), V((K4, S, P_, 2 * Y), f32),
            V((Q, g, 2 * B), f32), V((Q, g, 2 * B), f32),
            V((K4 // 2 * P_, 2 * B), f32),
            DMA((Q,)), DMA((Q,)), DMA((K4, S)), DMA((K4, S)),
            DMA((Q,)), DMA((Q,)), DMA((Q,)), DMA((Q,)),
            DMA((K4, S)), DMA((K4, S)), DMA((Q,)), DMA((Q,)),
        ],
        1, (spec, kern_here, target_here) + consts, 56,
    )
    resist = lax.ppermute(resist, ("space", "kern"), swap).T

    re, im = total[:, :B], total[:, B:]
    stacked = jnp.stack([jnp.stack([re, im], 1), jnp.stack([im, -re], 1)])
    stacked = stacked.reshape(2, g, 2, Q, nx, Q, g).transpose(0, 1, 3, 5, 4, 2, 6).reshape(2 * g, 2 * B)
    delta = jnp.dot(stacked, table, precision=high) * (1.0 / N)
    piece = call(
        functools.partial(gather_kernel, S, Q, R),
        jax.ShapeDtypeStruct((Q, S, 2 * g, R), f32), [vm],
        [DMA((S,)), DMA((S,)), DMA((S,)), DMA((S,)), DMA((2, S)), DMA((2, S)), DMA],
        2, (delta,), 16,
    )
    gradient = lax.dot_general(piece.reshape(2 * B, R), table, (((0,), (0,)), ((), ())), precision=high)
    return gradient, resist


def solution(mesh):
    in_specs = (P("space", None), P(None, "kern", "space", None), P("space", None))
    out_specs = (P("space", None), P("space", None))
    S, Q = mesh.shape["space"], mesh.shape["kern"]
    whole_tiles = Q == 4 and S % Q == 0 and (B // S // Q) % 16 == 0 and (G // S) % 128 == 0
    body = functools.partial(fast, S, Q) if whole_tiles else local
    return jax.shard_map(body, mesh=mesh, in_specs=in_specs, out_specs=out_specs, check_vma=False)
```

```python
import functools

import jax
import jax.numpy as jnp
import ml_dtypes
import numpy as np
from jax import lax
from jax.experimental import pallas as pl
from jax.experimental.pallas import tpu as pltpu
from jax.sharding import PartitionSpec as P

N = 4096
B = 512
G = 1024


steepness = 8.0
threshold = 1.5
highest = lax.Precision.HIGHEST
block_limit = 1024


def phases(left, right, modulus):
    product = left[:, None] * right[None, :] % modulus
    return product.astype(jnp.float32) * (2.0 * jnp.pi / modulus)


def column_table(pixels, frequency, length):
    angle = phases(pixels, frequency, length)
    return jnp.concatenate([jnp.cos(angle), -jnp.sin(angle)], axis=1)


def row_table(pixels, frequency, length):
    angle = phases(pixels, frequency, length)
    return jnp.concatenate([jnp.cos(angle), -jnp.sin(angle)], axis=1) / length


def grid_table(frequency, points):
    angle = phases(frequency, jnp.arange(points, dtype=jnp.int32), points)
    return jnp.concatenate([jnp.cos(angle), jnp.sin(angle)], axis=1)


def forward_columns(mask, frequency):
    rows = mask.shape[0]
    span = min(block_limit, N)
    count = frequency.shape[0]

    def step(index, running):
        start = index * span
        table = column_table(start + jnp.arange(span, dtype=jnp.int32), frequency, N)
        piece = lax.dynamic_slice_in_dim(mask, start, span, 1).astype(jnp.float32)
        return running + lax.dot_general(table, piece, (((0,), (1,)), ((), ())), precision=highest)

    running = lax.fori_loop(0, N // span, step, jnp.zeros((2 * count, rows), jnp.float32))
    return running.reshape(2, count, rows)


def forward_rows(arrived):
    count = arrived.shape[1]
    flat = arrived.reshape(2 * count, N)
    frequency = jnp.arange(B, dtype=jnp.int32) - B // 2
    span = min(block_limit, N)

    def step(index, running):
        start = index * span
        table = row_table(start + jnp.arange(span, dtype=jnp.int32), frequency, N)
        piece = lax.dynamic_slice_in_dim(flat, start, span, 1)
        return running + jnp.dot(piece, table, precision=highest)

    running = lax.fori_loop(0, N // span, step, jnp.zeros((2 * count, 2 * B), jnp.float32))
    real_part = running[:count, :B] - running[count:, B:]
    imag_part = running[:count, B:] + running[count:, :B]
    return jnp.stack([real_part, imag_part])


def adjoint_rows(sum_re, sum_im):
    count = sum_re.shape[0]
    stacked = jnp.concatenate(
        [jnp.concatenate([sum_re, sum_im], axis=1), jnp.concatenate([sum_im, -sum_re], axis=1)],
        axis=0,
    )
    frequency = jnp.arange(B, dtype=jnp.int32) - B // 2
    span = min(block_limit, N)

    def step(index, output):
        start = index * span
        table = row_table(start + jnp.arange(span, dtype=jnp.int32), frequency, N)
        piece = lax.dot_general(stacked, table, (((1,), (1,)), ((), ())), precision=highest)
        return lax.dynamic_update_slice_in_dim(output, piece, start, 1)

    output = lax.fori_loop(0, N // span, step, jnp.zeros((2 * count, N), jnp.float32))
    return output.reshape(2, count, N)


def add_columns(total, spectrum, frequency):
    span = min(block_limit, N)

    def step(index, running):
        start = index * span
        table = column_table(start + jnp.arange(span, dtype=jnp.int32), frequency, N)
        piece = lax.dot_general(spectrum, table, (((0,), (1,)), ((), ())), precision=highest)
        current = lax.dynamic_slice_in_dim(running, start, span, 1)
        return lax.dynamic_update_slice_in_dim(running, current + piece, start, 1)

    return lax.fori_loop(0, N // span, step, total)


def local(mask, kernels, target):
    rows = mask.shape[0]
    kern_count = lax.axis_size("kern")
    space_count = lax.axis_size("space")
    group = lax.axis_index("kern")
    per_space = B // space_count
    per_group = per_space // kern_count
    frequency = jnp.arange(B, dtype=jnp.int32) - B // 2
    subset = (
        per_space * jnp.arange(space_count, dtype=jnp.int32)[:, None]
        + per_group * group
        + jnp.arange(per_group, dtype=jnp.int32)[None, :]
    )
    columns = forward_columns(mask, subset.reshape(-1) - B // 2)
    arrived = lax.all_to_all(columns, "space", split_axis=1, concat_axis=2, tiled=True)
    spectrum = lax.all_gather(forward_rows(arrived), "kern", axis=1, tiled=True)
    kern_swap = jnp.swapaxes(kernels, 1, 2)
    kernel_count = kern_swap.shape[2]
    spec_re = spectrum[0][:, None, :]
    spec_im = spectrum[1][:, None, :]
    prod_re = kern_swap[0] * spec_re - kern_swap[1] * spec_im
    prod_im = kern_swap[0] * spec_im + kern_swap[1] * spec_re
    grid = grid_table(frequency, G)
    lifted = jnp.dot(
        jnp.stack([prod_re, prod_im]).reshape(2 * per_space * kernel_count, B),
        grid,
        precision=highest,
    )
    lifted = lifted.reshape(2, per_space, kernel_count, 2 * G)
    coarse_re = lifted[0, :, :, :G] - lifted[1, :, :, G:]
    coarse_im = lifted[0, :, :, G:] + lifted[1, :, :, :G]
    coarse = jnp.stack([coarse_re, coarse_im], axis=1)
    gathered = lax.all_to_all(coarse, "space", split_axis=3, concat_axis=0, tiled=True)
    grid_rows = gathered.shape[3]
    image = lax.dot_general(
        gathered.reshape(B, 2 * kernel_count * grid_rows),
        grid,
        (((0,), (0,)), ((), ())),
        precision=highest,
    )
    image = image.reshape(2, kernel_count, grid_rows, 2 * G)
    field_re = image[0, :, :, :G] - image[1, :, :, G:]
    field_im = image[0, :, :, G:] + image[1, :, :, :G]
    partial_light = jnp.sum(field_re * field_re + field_im * field_im, axis=0) / (B * B)
    intensity = lax.psum(partial_light, "kern")
    resist = jax.nn.sigmoid(steepness * (intensity - threshold))
    slope = 2.0 * (resist - target.astype(jnp.float32)) * steepness * resist * (1.0 - resist)
    scale = 2.0 * slope / (B * B)
    grad_re = scale * field_re
    grad_im = scale * field_im
    mixed = jnp.stack(
        [
            jnp.concatenate([grad_re, grad_im], axis=-1),
            jnp.concatenate([grad_im, -grad_re], axis=-1),
        ]
    )
    mixed = mixed.reshape(2 * kernel_count * grid_rows, 2 * G)
    backward = lax.dot_general(grid, mixed, (((1,), (1,)), ((), ())), precision=highest)
    backward = backward.reshape(B, 2, kernel_count, grid_rows)
    returned = lax.all_to_all(backward, "space", split_axis=0, concat_axis=3, tiled=True)
    back_re = returned[:, 0]
    back_im = returned[:, 1]
    mixed_two = jnp.stack(
        [
            jnp.concatenate([back_re, back_im], axis=-1),
            jnp.concatenate([back_im, -back_re], axis=-1),
        ]
    )
    mixed_two = mixed_two.reshape(2 * per_space * kernel_count, 2 * G)
    spectral = lax.dot_general(mixed_two, grid, (((1,), (1,)), ((), ())), precision=highest)
    spectral = spectral.reshape(2, per_space, kernel_count, B)
    sum_re = jnp.sum(kern_swap[0] * spectral[0] + kern_swap[1] * spectral[1], axis=1)
    sum_im = jnp.sum(kern_swap[0] * spectral[1] - kern_swap[1] * spectral[0], axis=1)
    empty = jnp.zeros((rows, N), jnp.float32)
    shares = (
        lax.psum_scatter(sum_re, "kern", scatter_dimension=0, tiled=True),
        lax.psum_scatter(sum_im, "kern", scatter_dimension=0, tiled=True),
    )
    delta = adjoint_rows(shares[0], shares[1])
    landed = lax.all_to_all(delta, "space", split_axis=2, concat_axis=1, tiled=True)
    ordering = (
        per_group * jnp.arange(kern_count, dtype=jnp.int32)[:, None, None]
        + per_space * jnp.arange(space_count, dtype=jnp.int32)[None, :, None]
        + jnp.arange(per_group, dtype=jnp.int32)[None, None, :]
    )
    ordered_freq = ordering.reshape(-1) - B // 2
    piece = lax.all_gather(landed, "kern", axis=1, tiled=True)
    width = piece.shape[1]
    gradient = add_columns(empty, piece.reshape(2 * width, rows), ordered_freq)
    return (gradient, resist)


MESH = pl.DeviceIdType.MESH


def split_constant(values):
    high = values.astype(np.float32).astype(ml_dtypes.bfloat16)
    low = (values - high.astype(np.float64)).astype(ml_dtypes.bfloat16)
    return jnp.asarray(high), jnp.asarray(low)


def pixel_table():
    f = np.arange(B) - B // 2
    angle = (f[:, None] * np.arange(N)) % N * (2 * np.pi / N)
    return jnp.asarray(np.concatenate([np.cos(angle), -np.sin(angle)]).astype(np.float32))


def coarse_tables(S):
    f = np.arange(B) - B // 2
    points = np.arange(G)
    angle = (f[:, None] * points[None, :]) % G * (2 * np.pi / G)
    c, s = np.cos(angle), np.sin(angle)
    Y = G // S
    cc = c.reshape(B, S, Y).transpose(1, 0, 2)
    ss = s.reshape(B, S, Y).transpose(1, 0, 2)
    lift = np.concatenate([np.concatenate([cc, ss], 2), np.concatenate([-ss, cc], 2)], 1)
    forward = np.concatenate([c.T, s.T], 0)
    backward = np.concatenate([c, s], 0)
    return split_constant(lift) + split_constant(forward) + split_constant(backward)


def halves(value):
    high = value.astype(jnp.bfloat16)
    return high, (value - high.astype(jnp.float32)).astype(jnp.bfloat16)


def dot3(ah, al, bh, bl, dims):
    d = functools.partial(lax.dot_general, dimension_numbers=(dims, ((), ())), preferred_element_type=jnp.float32)
    return d(ah, bh) + (d(al, bh) + d(ah, bl))


NN = ((1,), (0,))
NT = ((1,), (1,))


def remote(src, dst, send, recv, space, kern):
    return pltpu.make_async_remote_copy(
        src_ref=src, dst_ref=dst, send_sem=send, recv_sem=recv, device_id=(space, kern), device_id_type=MESH
    )


def imaging_kernel(
    S, Q, K4,
    part_ref, kern_mine, target_mine, lh_hbm, ll_hbm, fh_hbm, fl_hbm, bh_hbm, bl_hbm,
    out_ref, resist_ref,
    lh, ll, fh, fl, bh, bl, table_sem,
    kern_ref, target_ref, rbuf, specin, specq,
    specall, ph, pw, out1, in1, field, light, lightin, lightall, out2, in2, sums, rsin, acc,
    ps, pr_, ks, kr_, ts, tr, us, ur, gs, gr, cs, cr, zs, zr,
    spec_s, spec_r, s1, r1, ls, lr, as_, ar, s2, r2, rs, rr,
):
    nx, P_, Y = S // Q, B // S, G // S
    g = P_ // Q
    GQ = G // Q
    sp, kq = lax.axis_index("space"), lax.axis_index("kern")
    z, x = sp // nx, lax.rem(sp, nx)
    blk = kq * nx + x
    tables = [
        pltpu.make_async_copy(src, dst, table_sem.at[i])
        for i, (src, dst) in enumerate(
            zip((lh_hbm, ll_hbm, fh_hbm, fl_hbm, bh_hbm, bl_hbm), (lh, ll, fh, fl, bh, bl))
        )
    ]
    for t in tables:
        t.start()

    def member(o):
        b = lax.rem(blk + o, S)
        return b, z * nx + lax.rem(b, nx), b // nx

    def zpeer(o):
        q = lax.rem(z + o, Q)
        return q, q * nx + x

    barrier = pltpu.get_barrier_semaphore()
    swapped = z != kq

    def greet(o, c):
        pl.semaphore_signal(barrier, inc=1, device_id=(lax.rem(sp + o, S), kq), device_id_type=MESH)
        return c

    lax.fori_loop(1, S, greet, 0)
    for dk in range(1, Q):
        for xx in range(nx):
            pl.semaphore_signal(
                barrier, inc=1, device_id=(z * nx + xx, lax.rem(kq + dk, Q)), device_id_type=MESH
            )

    @pl.when(swapped)
    def _():
        pl.semaphore_signal(barrier, inc=1, device_id=(kq * nx + x, z), device_id_type=MESH)

    pl.semaphore_wait(barrier, S - 1 + (Q - 1) * nx + jnp.where(swapped, 1, 0))

    def part_copy(d, slot):
        return remote(part_ref.at[lax.rem(d, nx), d // nx], specin.at[slot], ps.at[d], pr_.at[slot], d, kq)

    def part_start(o, c):
        part_copy(lax.rem(sp + o, S), sp).start()
        return c

    lax.fori_loop(1, S, part_start, 0)
    specin[sp] = part_ref[x, z]

    def kern_copy(k):
        return remote(kern_mine.at[:, k], kern_ref.at[:, k], ks.at[k], kr_.at[k], kq * nx + x, z)

    target_copy = remote(target_mine, target_ref, ts, tr, kq * nx + x, z)

    @pl.when(swapped)
    def _():
        for k in range(K4):
            kern_copy(k).start()
        target_copy.start()

    @pl.when(jnp.logical_not(swapped))
    def _():
        kern_ref[...] = kern_mine[...]
        target_ref[...] = target_mine[...]

    def part_wait(o, c):
        d = lax.rem(sp + o, S)
        part_copy(d, d).wait()
        return c

    lax.fori_loop(1, S, part_wait, 0)
    total = specin[0]
    for d in range(1, S):
        total = total + specin[d]
    specq[...] = total

    def spec_copy(o, slot):
        q, s = zpeer(o)
        return remote(specq, specall.at[slot], spec_s.at[q], spec_r.at[slot], s, kq)

    for o in range(1, Q):
        spec_copy(o, z).start()
    specall[z] = total
    for o in range(1, Q):
        spec_copy(o, zpeer(o)[0]).wait()

    spec = specall[...].reshape(P_, 2 * B)
    sr, si = spec[:, :B], spec[:, B:]
    tables[0].wait()
    tables[1].wait()
    pair = K4 // 2

    def copy1(k, b, s, kk, slot):
        return remote(out1.at[k, b], in1.at[k, slot], s1.at[k, b], r1.at[k, slot], s, kk)

    for h in range(2):
        @pl.when(swapped)
        def _():
            for j in range(pair):
                kern_copy(h * pair + j).wait()

        for k in range(h * pair, h * pair + pair):
            kr, ki = kern_ref[0, k], kern_ref[1, k]
            rows = pl.ds(k * P_, P_)
            ph[rows, :B], pw[rows, :B] = halves(kr * sr - ki * si)
            ph[rows, B:], pw[rows, B:] = halves(kr * si + ki * sr)
        rows = pl.ds(h * pair * P_, pair * P_)

        def lift(b):
            return dot3(ph[rows, :], pw[rows, :], lh[b], ll[b], NN).reshape(pair, P_, 2 * Y)

        def step(o, c):
            b, s, kk = member(o)
            value = lift(b)
            for j in range(pair):
                out1[h * pair + j, b] = value[j]
            for j in range(pair):
                copy1(h * pair + j, b, s, kk, blk).start()
            return c

        lax.fori_loop(1, S, step, 0)
        value = lift(blk)
        for j in range(pair):
            in1[h * pair + j, blk] = value[j]

    for t in tables[2:]:
        t.wait()
    chunk = 256

    def image(k, c):
        def arrive(o, c):
            b, s, kk = member(o)
            copy1(k, b, s, kk, b).wait_recv()
            return c

        lax.fori_loop(1, S, arrive, 0)
        dh, dl = halves(in1[k].reshape(B, 2 * Y))

        def part(j, c):
            rows = pl.ds(pl.multiple_of(j * chunk, chunk), chunk)
            low = pl.ds(pl.multiple_of(G + j * chunk, chunk), chunk)
            a = dot3(fh[rows, :], fl[rows, :], dh, dl, NN)
            b = dot3(fh[low, :], fl[low, :], dh, dl, NN)
            re = a[:, :Y] - b[:, Y:]
            im = a[:, Y:] + b[:, :Y]
            field[k, rows, :Y] = re
            field[k, rows, Y:] = im
            power = re * re + im * im

            @pl.when(k == 0)
            def _():
                light[rows, :] = power

            @pl.when(k > 0)
            def _():
                light[rows, :] = light[rows, :] + power

            return c

        return lax.fori_loop(0, G // chunk, part, c)

    lax.fori_loop(0, K4, image, 0)

    quarter = lambda q: pl.ds(pl.multiple_of(q * GQ, GQ), GQ)

    def light_copy(o, slot):
        q, s = zpeer(o)
        return remote(light.at[quarter(q)], lightin.at[slot], ls.at[q], lr.at[slot], s, kq)

    for o in range(1, Q):
        light_copy(o, z).start()
    lightin[z] = light[quarter(z), :]
    for o in range(1, Q):
        light_copy(o, zpeer(o)[0]).wait()
    total = lightin[0]
    for q in range(1, Q):
        total = total + lightin[q]
    lightall[z] = total * (1.0 / (B * B))

    def all_copy(o, slot):
        q, s = zpeer(o)
        return remote(lightall.at[z], lightall.at[slot], as_.at[q], ar.at[slot], s, kq)

    for o in range(1, Q):
        all_copy(o, z).start()
    for o in range(1, Q):
        all_copy(o, zpeer(o)[0]).wait_recv()

    @pl.when(swapped)
    def _():
        target_copy.wait()

    for q in range(Q):
        rows = pl.ds(q * GQ, GQ)
        resist = jax.nn.sigmoid(steepness * (lightall[q] - threshold))
        rbuf[rows, :] = resist
        light[rows, :] = (4.0 * steepness / (B * B)) * (resist - target_ref[rows, :]) * resist * (1.0 - resist)

    resist_copy = remote(rbuf, resist_ref, us, ur, kq * nx + x, z)

    @pl.when(swapped)
    def _():
        resist_copy.start()

    @pl.when(jnp.logical_not(swapped))
    def _():
        resist_ref[...] = rbuf[...]

    def copy2(k, b, s, kk, slot):
        return remote(out2.at[k, b], in2.at[k, slot], s2.at[k, b], r2.at[k, slot], s, kk)

    def back(k, c):
        scale = light[...]
        scale = jnp.concatenate([scale, scale], axis=1)
        dh, dl = halves(field[k] * scale)

        def part(j, c):
            rows = pl.ds(pl.multiple_of(j * chunk, chunk), chunk)
            low = pl.ds(pl.multiple_of(B + j * chunk, chunk), chunk)
            a = dot3(bh[rows, :], bl[rows, :], dh, dl, NN)
            b = dot3(bh[low, :], bl[low, :], dh, dl, NN)
            value = jnp.concatenate([a[:, :Y] + b[:, Y:], a[:, Y:] - b[:, :Y]], axis=1)
            out2[k, pl.ds(j * (chunk // P_), chunk // P_)] = value.reshape(chunk // P_, P_, 2 * Y)
            return c

        lax.fori_loop(0, B // chunk, part, c)

        def launch(o, c):
            b, s, kk = member(o)
            copy2(k, b, s, kk, blk).start()
            return c

        lax.fori_loop(1, S, launch, 0)
        in2[k, blk] = out2[k, blk]
        return c

    lax.fori_loop(0, K4, back, 0)

    sum_re = jnp.zeros((P_, B), jnp.float32)
    sum_im = jnp.zeros((P_, B), jnp.float32)
    for h in range(2):
        for j in range(pair):
            def arrive2(o, c):
                b, s, kk = member(o)
                copy2(h * pair + j, b, s, kk, b).wait_recv()
                return c

            lax.fori_loop(1, S, arrive2, 0)
        acc[...] = jnp.zeros_like(acc)

        def add(s, c):
            dh, dl = halves(in2[pl.ds(h * pair, pair), s].reshape(pair * P_, 2 * Y))
            acc[...] += dot3(dh, dl, lh[s], ll[s], NT)
            return c

        lax.fori_loop(0, S, add, 0)
        for j in range(pair):
            k = h * pair + j
            kr, ki = kern_ref[0, k], kern_ref[1, k]
            pr, pi = acc[pl.ds(j * P_, P_), :B], acc[pl.ds(j * P_, P_), B:]
            sum_re = sum_re + kr * pr + ki * pi
            sum_im = sum_im + kr * pi - ki * pr
    sums[:, :, :B] = sum_re.reshape(Q, g, B)
    sums[:, :, B:] = sum_im.reshape(Q, g, B)

    def sum_copy(o, slot):
        q, s = zpeer(o)
        return remote(sums.at[q], rsin.at[slot], rs.at[q], rr.at[slot], s, kq)

    for o in range(1, Q):
        sum_copy(o, z).start()
    rsin[z] = sums[z]
    for o in range(1, Q):
        sum_copy(o, zpeer(o)[0]).wait()
    total = rsin[0]
    for q in range(1, Q):
        total = total + rsin[q]
    out_ref[blk, z] = total

    def z_copy(o, slot):
        q, s = zpeer(o)
        return remote(out_ref.at[blk, z], out_ref.at[blk, slot], zs.at[q], zr.at[slot], s, kq)

    def z_from(o):
        q, s = zpeer(o)
        return remote(out_ref.at[blk, q], out_ref.at[blk, q], zs.at[q], zr.at[q], s, kq)

    for o in range(1, Q):
        z_copy(o, z).start()
    for o in range(1, Q):
        z_from(o).wait_recv()
    kc = kq + 1 - 2 * lax.rem(kq, 2)
    others = []
    for dx in range(nx):
        for dy in range(2):
            if dx or dy:
                kk, xx = lax.rem(kq + 2 * dy, Q), lax.rem(x + dx, nx)
                xf = lax.rem(x + nx - dx, nx)
                others.append((kk, xx, kk * nx + xx, xf, kk * nx + xf))

    def to_core(b):
        return remote(out_ref.at[b], out_ref.at[b], cs.at[b], cr.at[b], sp, kc)

    def to_brick(other):
        kk, xx, b, xf, bf = other
        return remote(out_ref.at[blk], out_ref.at[blk], gs.at[b], gr.at[blk], z * nx + xx, kk)

    def from_brick(other):
        kk, xx, b, xf, bf = other
        return remote(out_ref.at[bf], out_ref.at[bf], gs.at[b], gr.at[bf], z * nx + xf, kk)

    for other in others:
        to_brick(other).start()
    to_core(blk).start()
    for other in others:
        from_brick(other).wait_recv()
        to_core(other[4]).start()
    for kk, xx in [(kq, x)] + [(o[0], o[3]) for o in others]:
        mine = kk * nx + xx
        theirs = (kk + 1 - 2 * lax.rem(kk, 2)) * nx + xx
        to_core(mine).wait_send()
        to_core(theirs).wait_recv()
    for other in others:
        to_brick(other).wait_send()
    for o in range(1, Q):
        z_copy(o, z).wait_send()

    @pl.when(swapped)
    def _():
        resist_copy.wait()

    for o in range(1, Q):
        all_copy(o, z).wait_send()

    def drain(k, c):
        def one(o, c):
            b, s, kk = member(o)
            copy1(k, b, s, kk, blk).wait_send()
            copy2(k, b, s, kk, blk).wait_send()
            return c

        return lax.fori_loop(1, S, one, c)

    lax.fori_loop(0, K4, drain, 0)


def call(kernel, outs, specs, scratch, cid, args, mib):
    vm = pl.BlockSpec(memory_space=pltpu.VMEM)
    return pl.pallas_call(
        kernel,
        out_shape=outs,
        in_specs=specs,
        out_specs=jax.tree.map(lambda _: vm, outs),
        scratch_shapes=scratch,
        compiler_params=pltpu.CompilerParams(
            collective_id=cid, has_side_effects=True, vmem_limit_bytes=mib * 2**20
        ),
    )(*args)


def fast(S, Q, mask, kernels, target):
    f32, bf16 = jnp.float32, jnp.bfloat16
    nx, P_, Y, R = S // Q, B // S, G // S, N // S
    g, K4 = P_ // Q, kernels.shape[1]
    DMA = pltpu.SemaphoreType.DMA
    vm, any_ = pl.BlockSpec(memory_space=pltpu.VMEM), pl.BlockSpec(memory_space=pl.ANY)
    high = lax.Precision.HIGH
    sp, kq = lax.axis_index("space"), lax.axis_index("kern")
    table = pixel_table()
    C = B // Q

    rows = jnp.concatenate([lax.dynamic_slice_in_dim(table, part * B + kq * C, C, 0) for part in range(2)], axis=0)
    columns = lax.dot_general(rows, mask.astype(f32), (((1,), (1,)), ((), ())), precision=high)
    slab = lax.dynamic_slice_in_dim(table, sp * R, R, 1) * (1.0 / N)
    t = lax.dot_general(columns, slab, (((1,), (1,)), ((), ())), precision=high)
    part = jnp.concatenate([t[:C, :B] - t[C:, B:], t[:C, B:] + t[C:, :B]], axis=1)

    consts = coarse_tables(S)
    V = pltpu.VMEM
    total, resist = call(
        functools.partial(imaging_kernel, S, Q, K4),
        (jax.ShapeDtypeStruct((S, Q, g, 2 * B), f32), jax.ShapeDtypeStruct((G, Y), f32)),
        [vm, vm, vm] + [any_] * 6,
        [V(c.shape, bf16) for c in consts] + [DMA((6,))] + [
            V((2, K4, P_, B), f32), V((G, Y), f32), V((G, Y), f32),
            V((S, g, 2 * B), f32), V((g, 2 * B), f32),
            V((Q, g, 2 * B), f32),
            V((K4 * P_, 2 * B), bf16), V((K4 * P_, 2 * B), bf16),
            V((K4, S, P_, 2 * Y), f32), V((K4, S, P_, 2 * Y), f32),
            V((K4, G, 2 * Y), f32), V((G, Y), f32),
            V((Q, G // Q, Y), f32), V((Q, G // Q, Y), f32),
            V((K4, S, P_, 2 * Y), f32), V((K4, S, P_, 2 * Y), f32),
            V((Q, g, 2 * B), f32), V((Q, g, 2 * B), f32),
            V((K4 // 2 * P_, 2 * B), f32),
            DMA((S,)), DMA((S,)), DMA((K4,)), DMA((K4,)), DMA, DMA, DMA, DMA,
            DMA((S,)), DMA((S,)), DMA((S,)), DMA((S,)), DMA((Q,)), DMA((Q,)),
            DMA((Q,)), DMA((Q,)), DMA((K4, S)), DMA((K4, S)),
            DMA((Q,)), DMA((Q,)), DMA((Q,)), DMA((Q,)),
            DMA((K4, S)), DMA((K4, S)), DMA((Q,)), DMA((Q,)),
        ],
        1, (part.reshape(nx, Q, g, 2 * B), kernels, target.T.astype(f32)) + consts, 58,
    )

    total = total.reshape(B, 2 * B)
    a, b = slab[:B], slab[B:]
    delta = jnp.concatenate([
        jnp.dot(total, slab, precision=high),
        jnp.dot(total, jnp.concatenate([-b, a], axis=0), precision=high),
    ], axis=0)
    gradient = lax.dot_general(lax.optimization_barrier(delta), table, (((0,), (0,)), ((), ())), precision=high)
    return gradient, resist.T


def solution(mesh):
    in_specs = (P("space", None), P(None, "kern", "space", None), P("space", None))
    out_specs = (P("space", None), P("space", None))
    S, Q = mesh.shape["space"], mesh.shape["kern"]
    whole_tiles = Q == 4 and S % Q == 0 and (B // S // Q) % 16 == 0 and (G // S) % 128 == 0
    body = functools.partial(fast, S, Q) if whole_tiles else local
    return jax.shard_map(body, mesh=mesh, in_specs=in_specs, out_specs=out_specs, check_vma=False)
```

```python
import functools

import jax
import jax.numpy as jnp
import ml_dtypes
import numpy as np
from jax import lax
from jax.experimental import pallas as pl
from jax.experimental.pallas import tpu as pltpu
from jax.sharding import PartitionSpec as P

N = 4096
B = 512
G = 1024


steepness = 8.0
threshold = 1.5
highest = lax.Precision.HIGHEST
block_limit = 1024


def phases(left, right, modulus):
    product = left[:, None] * right[None, :] % modulus
    return product.astype(jnp.float32) * (2.0 * jnp.pi / modulus)


def column_table(pixels, frequency, length):
    angle = phases(pixels, frequency, length)
    return jnp.concatenate([jnp.cos(angle), -jnp.sin(angle)], axis=1)


def row_table(pixels, frequency, length):
    angle = phases(pixels, frequency, length)
    return jnp.concatenate([jnp.cos(angle), -jnp.sin(angle)], axis=1) / length


def grid_table(frequency, points):
    angle = phases(frequency, jnp.arange(points, dtype=jnp.int32), points)
    return jnp.concatenate([jnp.cos(angle), jnp.sin(angle)], axis=1)


def forward_columns(mask, frequency):
    rows = mask.shape[0]
    span = min(block_limit, N)
    count = frequency.shape[0]

    def step(index, running):
        start = index * span
        table = column_table(start + jnp.arange(span, dtype=jnp.int32), frequency, N)
        piece = lax.dynamic_slice_in_dim(mask, start, span, 1).astype(jnp.float32)
        return running + lax.dot_general(table, piece, (((0,), (1,)), ((), ())), precision=highest)

    running = lax.fori_loop(0, N // span, step, jnp.zeros((2 * count, rows), jnp.float32))
    return running.reshape(2, count, rows)


def forward_rows(arrived):
    count = arrived.shape[1]
    flat = arrived.reshape(2 * count, N)
    frequency = jnp.arange(B, dtype=jnp.int32) - B // 2
    span = min(block_limit, N)

    def step(index, running):
        start = index * span
        table = row_table(start + jnp.arange(span, dtype=jnp.int32), frequency, N)
        piece = lax.dynamic_slice_in_dim(flat, start, span, 1)
        return running + jnp.dot(piece, table, precision=highest)

    running = lax.fori_loop(0, N // span, step, jnp.zeros((2 * count, 2 * B), jnp.float32))
    real_part = running[:count, :B] - running[count:, B:]
    imag_part = running[:count, B:] + running[count:, :B]
    return jnp.stack([real_part, imag_part])


def adjoint_rows(sum_re, sum_im):
    count = sum_re.shape[0]
    stacked = jnp.concatenate(
        [jnp.concatenate([sum_re, sum_im], axis=1), jnp.concatenate([sum_im, -sum_re], axis=1)],
        axis=0,
    )
    frequency = jnp.arange(B, dtype=jnp.int32) - B // 2
    span = min(block_limit, N)

    def step(index, output):
        start = index * span
        table = row_table(start + jnp.arange(span, dtype=jnp.int32), frequency, N)
        piece = lax.dot_general(stacked, table, (((1,), (1,)), ((), ())), precision=highest)
        return lax.dynamic_update_slice_in_dim(output, piece, start, 1)

    output = lax.fori_loop(0, N // span, step, jnp.zeros((2 * count, N), jnp.float32))
    return output.reshape(2, count, N)


def add_columns(total, spectrum, frequency):
    span = min(block_limit, N)

    def step(index, running):
        start = index * span
        table = column_table(start + jnp.arange(span, dtype=jnp.int32), frequency, N)
        piece = lax.dot_general(spectrum, table, (((0,), (1,)), ((), ())), precision=highest)
        current = lax.dynamic_slice_in_dim(running, start, span, 1)
        return lax.dynamic_update_slice_in_dim(running, current + piece, start, 1)

    return lax.fori_loop(0, N // span, step, total)


def local(mask, kernels, target):
    rows = mask.shape[0]
    kern_count = lax.axis_size("kern")
    space_count = lax.axis_size("space")
    group = lax.axis_index("kern")
    per_space = B // space_count
    per_group = per_space // kern_count
    frequency = jnp.arange(B, dtype=jnp.int32) - B // 2
    subset = (
        per_space * jnp.arange(space_count, dtype=jnp.int32)[:, None]
        + per_group * group
        + jnp.arange(per_group, dtype=jnp.int32)[None, :]
    )
    columns = forward_columns(mask, subset.reshape(-1) - B // 2)
    arrived = lax.all_to_all(columns, "space", split_axis=1, concat_axis=2, tiled=True)
    spectrum = lax.all_gather(forward_rows(arrived), "kern", axis=1, tiled=True)
    kern_swap = jnp.swapaxes(kernels, 1, 2)
    kernel_count = kern_swap.shape[2]
    spec_re = spectrum[0][:, None, :]
    spec_im = spectrum[1][:, None, :]
    prod_re = kern_swap[0] * spec_re - kern_swap[1] * spec_im
    prod_im = kern_swap[0] * spec_im + kern_swap[1] * spec_re
    grid = grid_table(frequency, G)
    lifted = jnp.dot(
        jnp.stack([prod_re, prod_im]).reshape(2 * per_space * kernel_count, B),
        grid,
        precision=highest,
    )
    lifted = lifted.reshape(2, per_space, kernel_count, 2 * G)
    coarse_re = lifted[0, :, :, :G] - lifted[1, :, :, G:]
    coarse_im = lifted[0, :, :, G:] + lifted[1, :, :, :G]
    coarse = jnp.stack([coarse_re, coarse_im], axis=1)
    gathered = lax.all_to_all(coarse, "space", split_axis=3, concat_axis=0, tiled=True)
    grid_rows = gathered.shape[3]
    image = lax.dot_general(
        gathered.reshape(B, 2 * kernel_count * grid_rows),
        grid,
        (((0,), (0,)), ((), ())),
        precision=highest,
    )
    image = image.reshape(2, kernel_count, grid_rows, 2 * G)
    field_re = image[0, :, :, :G] - image[1, :, :, G:]
    field_im = image[0, :, :, G:] + image[1, :, :, :G]
    partial_light = jnp.sum(field_re * field_re + field_im * field_im, axis=0) / (B * B)
    intensity = lax.psum(partial_light, "kern")
    resist = jax.nn.sigmoid(steepness * (intensity - threshold))
    slope = 2.0 * (resist - target.astype(jnp.float32)) * steepness * resist * (1.0 - resist)
    scale = 2.0 * slope / (B * B)
    grad_re = scale * field_re
    grad_im = scale * field_im
    mixed = jnp.stack(
        [
            jnp.concatenate([grad_re, grad_im], axis=-1),
            jnp.concatenate([grad_im, -grad_re], axis=-1),
        ]
    )
    mixed = mixed.reshape(2 * kernel_count * grid_rows, 2 * G)
    backward = lax.dot_general(grid, mixed, (((1,), (1,)), ((), ())), precision=highest)
    backward = backward.reshape(B, 2, kernel_count, grid_rows)
    returned = lax.all_to_all(backward, "space", split_axis=0, concat_axis=3, tiled=True)
    back_re = returned[:, 0]
    back_im = returned[:, 1]
    mixed_two = jnp.stack(
        [
            jnp.concatenate([back_re, back_im], axis=-1),
            jnp.concatenate([back_im, -back_re], axis=-1),
        ]
    )
    mixed_two = mixed_two.reshape(2 * per_space * kernel_count, 2 * G)
    spectral = lax.dot_general(mixed_two, grid, (((1,), (1,)), ((), ())), precision=highest)
    spectral = spectral.reshape(2, per_space, kernel_count, B)
    sum_re = jnp.sum(kern_swap[0] * spectral[0] + kern_swap[1] * spectral[1], axis=1)
    sum_im = jnp.sum(kern_swap[0] * spectral[1] - kern_swap[1] * spectral[0], axis=1)
    empty = jnp.zeros((rows, N), jnp.float32)
    shares = (
        lax.psum_scatter(sum_re, "kern", scatter_dimension=0, tiled=True),
        lax.psum_scatter(sum_im, "kern", scatter_dimension=0, tiled=True),
    )
    delta = adjoint_rows(shares[0], shares[1])
    landed = lax.all_to_all(delta, "space", split_axis=2, concat_axis=1, tiled=True)
    ordering = (
        per_group * jnp.arange(kern_count, dtype=jnp.int32)[:, None, None]
        + per_space * jnp.arange(space_count, dtype=jnp.int32)[None, :, None]
        + jnp.arange(per_group, dtype=jnp.int32)[None, None, :]
    )
    ordered_freq = ordering.reshape(-1) - B // 2
    piece = lax.all_gather(landed, "kern", axis=1, tiled=True)
    width = piece.shape[1]
    gradient = add_columns(empty, piece.reshape(2 * width, rows), ordered_freq)
    return (gradient, resist)


MESH = pl.DeviceIdType.MESH


def split_constant(values):
    high = values.astype(np.float32).astype(ml_dtypes.bfloat16)
    low = (values - high.astype(np.float64)).astype(ml_dtypes.bfloat16)
    return jnp.asarray(high), jnp.asarray(low)


def pixel_table():
    f = np.arange(B) - B // 2
    angle = (f[:, None] * np.arange(N)) % N * (2 * np.pi / N)
    return jnp.asarray(np.concatenate([np.cos(angle), -np.sin(angle)]).astype(np.float32))


def coarse_tables(S):
    f = np.arange(B) - B // 2
    points = np.arange(G)
    angle = (f[:, None] * points[None, :]) % G * (2 * np.pi / G)
    c, s = np.cos(angle), np.sin(angle)
    Y = G // S
    cc = c.reshape(B, S, Y).transpose(1, 0, 2)
    ss = s.reshape(B, S, Y).transpose(1, 0, 2)
    lift = np.concatenate([np.concatenate([cc, ss], 2), np.concatenate([-ss, cc], 2)], 1)
    forward = np.concatenate([c.T, s.T], 0)
    backward = np.concatenate([c, s], 0)
    return split_constant(lift) + split_constant(forward) + split_constant(backward)


def halves(value):
    high = value.astype(jnp.bfloat16)
    return high, (value - high.astype(jnp.float32)).astype(jnp.bfloat16)


def dot3(ah, al, bh, bl, dims):
    d = functools.partial(lax.dot_general, dimension_numbers=(dims, ((), ())), preferred_element_type=jnp.float32)
    return d(ah, bh) + (d(al, bh) + d(ah, bl))


NN = ((1,), (0,))
NT = ((1,), (1,))


def remote(src, dst, send, recv, space, kern):
    return pltpu.make_async_remote_copy(
        src_ref=src, dst_ref=dst, send_sem=send, recv_sem=recv, device_id=(space, kern), device_id_type=MESH
    )


def crossed(v):
    return 2 * lax.rem(v, 2) + v // 2


def imaging_kernel(
    S, Q, K4,
    part_ref, kern_mine, target_mine, lh_hbm, ll_hbm, fh_hbm, fl_hbm, bh_hbm, bl_hbm,
    out_ref, resist_ref,
    lh, ll, fh, fl, bh, bl, table_sem,
    kern_ref, target_ref, rbuf, specin, specq,
    specall, ph, pw, out1, in1, field, light, lightin, lightall, out2, in2, sums, rsin, acc,
    ps, pr_, ks, kr_, ts, tr, us, ur, gs, gr, cs, cr, zs, zr,
    spec_s, spec_r, s1, r1, ls, lr, as_, ar, s2, r2, rs, rr,
):
    nx, P_, Y = S // Q, B // S, G // S
    g = P_ // Q
    GQ = G // Q
    sp, kq = lax.axis_index("space"), lax.axis_index("kern")
    z, x = sp // nx, lax.rem(sp, nx)
    blk = crossed(kq) * nx + x
    tables = [
        pltpu.make_async_copy(src, dst, table_sem.at[i])
        for i, (src, dst) in enumerate(
            zip((lh_hbm, ll_hbm, fh_hbm, fl_hbm, bh_hbm, bl_hbm), (lh, ll, fh, fl, bh, bl))
        )
    ]
    for t in tables:
        t.start()

    def member(o):
        b = lax.rem(blk + o, S)
        return b, z * nx + lax.rem(b, nx), crossed(b // nx)

    def zpeer(o):
        q = lax.rem(z + o, Q)
        return q, q * nx + x

    barrier = pltpu.get_barrier_semaphore()
    swapped = z != crossed(kq)
    partner = (crossed(kq) * nx + x, crossed(z))

    def greet(o, c):
        pl.semaphore_signal(barrier, inc=1, device_id=(lax.rem(sp + o, S), kq), device_id_type=MESH)
        return c

    lax.fori_loop(1, S, greet, 0)
    for dk in range(1, Q):
        for xx in range(nx):
            pl.semaphore_signal(
                barrier, inc=1, device_id=(z * nx + xx, lax.rem(kq + dk, Q)), device_id_type=MESH
            )

    @pl.when(swapped)
    def _():
        pl.semaphore_signal(barrier, inc=1, device_id=partner, device_id_type=MESH)

    pl.semaphore_wait(barrier, S - 1 + (Q - 1) * nx + jnp.where(swapped, 1, 0))

    def part_copy(d, slot):
        return remote(part_ref.at[lax.rem(d, nx), d // nx], specin.at[slot], ps.at[d], pr_.at[slot], d, kq)

    def part_start(o, c):
        part_copy(lax.rem(sp + o, S), sp).start()
        return c

    lax.fori_loop(1, S, part_start, 0)
    specin[sp] = part_ref[x, z]

    def kern_copy(k):
        return remote(kern_mine.at[:, k], kern_ref.at[:, k], ks.at[k], kr_.at[k], *partner)

    target_copy = remote(target_mine, target_ref, ts, tr, *partner)

    @pl.when(swapped)
    def _():
        for k in range(K4):
            kern_copy(k).start()
        target_copy.start()

    @pl.when(jnp.logical_not(swapped))
    def _():
        kern_ref[...] = kern_mine[...]
        target_ref[...] = target_mine[...]

    def part_wait(o, c):
        d = lax.rem(sp + o, S)
        part_copy(d, d).wait()
        return c

    lax.fori_loop(1, S, part_wait, 0)
    total = specin[0]
    for d in range(1, S):
        total = total + specin[d]
    specq[...] = total

    def spec_copy(o, slot):
        q, s = zpeer(o)
        return remote(specq, specall.at[slot], spec_s.at[q], spec_r.at[slot], s, kq)

    for o in range(1, Q):
        spec_copy(o, z).start()
    specall[z] = total
    for o in range(1, Q):
        spec_copy(o, zpeer(o)[0]).wait()

    spec = specall[...].reshape(P_, 2 * B)
    sr, si = spec[:, :B], spec[:, B:]
    tables[0].wait()
    tables[1].wait()
    pair = K4 // 2

    def copy1(k, b, s, kk, slot):
        return remote(out1.at[k, b], in1.at[k, slot], s1.at[k, b], r1.at[k, slot], s, kk)

    for h in range(2):
        @pl.when(swapped)
        def _():
            for j in range(pair):
                kern_copy(h * pair + j).wait()

        for k in range(h * pair, h * pair + pair):
            kr, ki = kern_ref[0, k], kern_ref[1, k]
            rows = pl.ds(k * P_, P_)
            ph[rows, :B], pw[rows, :B] = halves(kr * sr - ki * si)
            ph[rows, B:], pw[rows, B:] = halves(kr * si + ki * sr)
        rows = pl.ds(h * pair * P_, pair * P_)

        def lift(b):
            return dot3(ph[rows, :], pw[rows, :], lh[b], ll[b], NN).reshape(pair, P_, 2 * Y)

        def step(o, c):
            b, s, kk = member(o)
            value = lift(b)
            for j in range(pair):
                out1[h * pair + j, b] = value[j]
            for j in range(pair):
                copy1(h * pair + j, b, s, kk, blk).start()
            return c

        lax.fori_loop(1, S, step, 0)
        value = lift(blk)
        for j in range(pair):
            in1[h * pair + j, blk] = value[j]

    for t in tables[2:]:
        t.wait()
    chunk = 256

    def image(k, c):
        def arrive(o, c):
            b, s, kk = member(o)
            copy1(k, b, s, kk, b).wait_recv()
            return c

        lax.fori_loop(1, S, arrive, 0)
        dh, dl = halves(in1[k].reshape(B, 2 * Y))

        def part(j, c):
            rows = pl.ds(pl.multiple_of(j * chunk, chunk), chunk)
            low = pl.ds(pl.multiple_of(G + j * chunk, chunk), chunk)
            a = dot3(fh[rows, :], fl[rows, :], dh, dl, NN)
            b = dot3(fh[low, :], fl[low, :], dh, dl, NN)
            re = a[:, :Y] - b[:, Y:]
            im = a[:, Y:] + b[:, :Y]
            field[k, rows, :Y] = re
            field[k, rows, Y:] = im
            power = re * re + im * im

            @pl.when(k == 0)
            def _():
                light[rows, :] = power

            @pl.when(k > 0)
            def _():
                light[rows, :] = light[rows, :] + power

            return c

        return lax.fori_loop(0, G // chunk, part, c)

    lax.fori_loop(0, K4, image, 0)

    quarter = lambda q: pl.ds(pl.multiple_of(q * GQ, GQ), GQ)

    def light_copy(o, slot):
        q, s = zpeer(o)
        return remote(light.at[quarter(q)], lightin.at[slot], ls.at[q], lr.at[slot], s, kq)

    for o in range(1, Q):
        light_copy(o, z).start()
    lightin[z] = light[quarter(z), :]
    for o in range(1, Q):
        light_copy(o, zpeer(o)[0]).wait()
    total = lightin[0]
    for q in range(1, Q):
        total = total + lightin[q]
    lightall[z] = total * (1.0 / (B * B))

    def all_copy(o, slot):
        q, s = zpeer(o)
        return remote(lightall.at[z], lightall.at[slot], as_.at[q], ar.at[slot], s, kq)

    for o in range(1, Q):
        all_copy(o, z).start()
    for o in range(1, Q):
        all_copy(o, zpeer(o)[0]).wait_recv()

    @pl.when(swapped)
    def _():
        target_copy.wait()

    for q in range(Q):
        rows = pl.ds(q * GQ, GQ)
        resist = jax.nn.sigmoid(steepness * (lightall[q] - threshold))
        rbuf[rows, :] = resist
        light[rows, :] = (4.0 * steepness / (B * B)) * (resist - target_ref[rows, :]) * resist * (1.0 - resist)

    resist_copy = remote(rbuf, resist_ref, us, ur, *partner)

    @pl.when(swapped)
    def _():
        resist_copy.start()

    @pl.when(jnp.logical_not(swapped))
    def _():
        resist_ref[...] = rbuf[...]

    def copy2(k, b, s, kk, slot):
        return remote(out2.at[k, b], in2.at[k, slot], s2.at[k, b], r2.at[k, slot], s, kk)

    def back(k, c):
        scale = light[...]
        scale = jnp.concatenate([scale, scale], axis=1)
        dh, dl = halves(field[k] * scale)

        def part(j, c):
            rows = pl.ds(pl.multiple_of(j * chunk, chunk), chunk)
            low = pl.ds(pl.multiple_of(B + j * chunk, chunk), chunk)
            a = dot3(bh[rows, :], bl[rows, :], dh, dl, NN)
            b = dot3(bh[low, :], bl[low, :], dh, dl, NN)
            value = jnp.concatenate([a[:, :Y] + b[:, Y:], a[:, Y:] - b[:, :Y]], axis=1)
            out2[k, pl.ds(j * (chunk // P_), chunk // P_)] = value.reshape(chunk // P_, P_, 2 * Y)
            return c

        lax.fori_loop(0, B // chunk, part, c)

        def launch(o, c):
            b, s, kk = member(o)
            copy2(k, b, s, kk, blk).start()
            return c

        lax.fori_loop(1, S, launch, 0)
        in2[k, blk] = out2[k, blk]
        return c

    lax.fori_loop(0, K4, back, 0)

    sum_re = jnp.zeros((P_, B), jnp.float32)
    sum_im = jnp.zeros((P_, B), jnp.float32)
    for h in range(2):
        for j in range(pair):
            def arrive2(o, c):
                b, s, kk = member(o)
                copy2(h * pair + j, b, s, kk, b).wait_recv()
                return c

            lax.fori_loop(1, S, arrive2, 0)
        acc[...] = jnp.zeros_like(acc)

        def add(s, c):
            dh, dl = halves(in2[pl.ds(h * pair, pair), s].reshape(pair * P_, 2 * Y))
            acc[...] += dot3(dh, dl, lh[s], ll[s], NT)
            return c

        lax.fori_loop(0, S, add, 0)
        for j in range(pair):
            k = h * pair + j
            kr, ki = kern_ref[0, k], kern_ref[1, k]
            pr, pi = acc[pl.ds(j * P_, P_), :B], acc[pl.ds(j * P_, P_), B:]
            sum_re = sum_re + kr * pr + ki * pi
            sum_im = sum_im + kr * pi - ki * pr
    sums[:, :, :B] = sum_re.reshape(Q, g, B)
    sums[:, :, B:] = sum_im.reshape(Q, g, B)

    def sum_copy(o, slot):
        q, s = zpeer(o)
        return remote(sums.at[q], rsin.at[slot], rs.at[q], rr.at[slot], s, kq)

    for o in range(1, Q):
        sum_copy(o, z).start()
    rsin[z] = sums[z]
    for o in range(1, Q):
        sum_copy(o, zpeer(o)[0]).wait()
    total = rsin[0]
    for q in range(1, Q):
        total = total + rsin[q]
    out_ref[blk, z] = total

    def z_copy(o, slot):
        q, s = zpeer(o)
        return remote(out_ref.at[blk, z], out_ref.at[blk, slot], zs.at[q], zr.at[slot], s, kq)

    def z_from(o):
        q, s = zpeer(o)
        return remote(out_ref.at[blk, q], out_ref.at[blk, q], zs.at[q], zr.at[q], s, kq)

    for o in range(1, Q):
        z_copy(o, z).start()
    for o in range(1, Q):
        z_from(o).wait_recv()
    kc = kq + 1 - 2 * lax.rem(kq, 2)
    others = []
    for dx in range(nx):
        for dy in range(2):
            if dx or dy:
                kk, xx = lax.rem(kq + 2 * dy, Q), lax.rem(x + dx, nx)
                xf = lax.rem(x + nx - dx, nx)
                others.append((kk, xx, crossed(kk) * nx + xx, xf, crossed(kk) * nx + xf))

    def to_core(b):
        return remote(out_ref.at[b], out_ref.at[b], cs.at[b], cr.at[b], sp, kc)

    def to_brick(other):
        kk, xx, b, xf, bf = other
        return remote(out_ref.at[blk], out_ref.at[blk], gs.at[b], gr.at[blk], z * nx + xx, kk)

    def from_brick(other):
        kk, xx, b, xf, bf = other
        return remote(out_ref.at[bf], out_ref.at[bf], gs.at[b], gr.at[bf], z * nx + xf, kk)

    for other in others:
        to_brick(other).start()
    to_core(blk).start()
    for other in others:
        from_brick(other).wait_recv()
        to_core(other[4]).start()
    for kk, xx in [(kq, x)] + [(o[0], o[3]) for o in others]:
        mine = crossed(kk) * nx + xx
        theirs = crossed(kk + 1 - 2 * lax.rem(kk, 2)) * nx + xx
        to_core(mine).wait_send()
        to_core(theirs).wait_recv()
    for other in others:
        to_brick(other).wait_send()
    for o in range(1, Q):
        z_copy(o, z).wait_send()

    @pl.when(swapped)
    def _():
        resist_copy.wait()

    for o in range(1, Q):
        all_copy(o, z).wait_send()

    def drain(k, c):
        def one(o, c):
            b, s, kk = member(o)
            copy1(k, b, s, kk, blk).wait_send()
            copy2(k, b, s, kk, blk).wait_send()
            return c

        return lax.fori_loop(1, S, one, c)

    lax.fori_loop(0, K4, drain, 0)


def call(kernel, outs, specs, scratch, cid, args, mib):
    vm = pl.BlockSpec(memory_space=pltpu.VMEM)
    return pl.pallas_call(
        kernel,
        out_shape=outs,
        in_specs=specs,
        out_specs=jax.tree.map(lambda _: vm, outs),
        scratch_shapes=scratch,
        compiler_params=pltpu.CompilerParams(
            collective_id=cid, has_side_effects=True, vmem_limit_bytes=mib * 2**20
        ),
    )(*args)


def fast(S, Q, mask, kernels, target):
    f32, bf16 = jnp.float32, jnp.bfloat16
    nx, P_, Y, R = S // Q, B // S, G // S, N // S
    g, K4 = P_ // Q, kernels.shape[1]
    DMA = pltpu.SemaphoreType.DMA
    vm, any_ = pl.BlockSpec(memory_space=pltpu.VMEM), pl.BlockSpec(memory_space=pl.ANY)
    high = lax.Precision.HIGH
    sp, kq = lax.axis_index("space"), lax.axis_index("kern")
    table = pixel_table()
    C = B // Q

    rows = jnp.concatenate([lax.dynamic_slice_in_dim(table, part * B + crossed(kq) * C, C, 0) for part in range(2)], axis=0)
    columns = lax.dot_general(rows, mask.astype(f32), (((1,), (1,)), ((), ())), precision=high)
    slab = lax.dynamic_slice_in_dim(table, sp * R, R, 1) * (1.0 / N)
    t = lax.dot_general(columns, slab, (((1,), (1,)), ((), ())), precision=high)
    part = jnp.concatenate([t[:C, :B] - t[C:, B:], t[:C, B:] + t[C:, :B]], axis=1)

    consts = coarse_tables(S)
    V = pltpu.VMEM
    total, resist = call(
        functools.partial(imaging_kernel, S, Q, K4),
        (jax.ShapeDtypeStruct((S, Q, g, 2 * B), f32), jax.ShapeDtypeStruct((G, Y), f32)),
        [vm, vm, vm] + [any_] * 6,
        [V(c.shape, bf16) for c in consts] + [DMA((6,))] + [
            V((2, K4, P_, B), f32), V((G, Y), f32), V((G, Y), f32),
            V((S, g, 2 * B), f32), V((g, 2 * B), f32),
            V((Q, g, 2 * B), f32),
            V((K4 * P_, 2 * B), bf16), V((K4 * P_, 2 * B), bf16),
            V((K4, S, P_, 2 * Y), f32), V((K4, S, P_, 2 * Y), f32),
            V((K4, G, 2 * Y), f32), V((G, Y), f32),
            V((Q, G // Q, Y), f32), V((Q, G // Q, Y), f32),
            V((K4, S, P_, 2 * Y), f32), V((K4, S, P_, 2 * Y), f32),
            V((Q, g, 2 * B), f32), V((Q, g, 2 * B), f32),
            V((K4 // 2 * P_, 2 * B), f32),
            DMA((S,)), DMA((S,)), DMA((K4,)), DMA((K4,)), DMA, DMA, DMA, DMA,
            DMA((S,)), DMA((S,)), DMA((S,)), DMA((S,)), DMA((Q,)), DMA((Q,)),
            DMA((Q,)), DMA((Q,)), DMA((K4, S)), DMA((K4, S)),
            DMA((Q,)), DMA((Q,)), DMA((Q,)), DMA((Q,)),
            DMA((K4, S)), DMA((K4, S)), DMA((Q,)), DMA((Q,)),
        ],
        1, (part.reshape(nx, Q, g, 2 * B), kernels, target.T.astype(f32)) + consts, 58,
    )

    total = total.reshape(B, 2 * B)
    a, b = slab[:B], slab[B:]
    delta = jnp.concatenate([
        jnp.dot(total, slab, precision=high),
        jnp.dot(total, jnp.concatenate([-b, a], axis=0), precision=high),
    ], axis=0)
    gradient = lax.dot_general(lax.optimization_barrier(delta), table, (((0,), (0,)), ((), ())), precision=high)
    return gradient, resist.T


def solution(mesh):
    in_specs = (P("space", None), P(None, "kern", "space", None), P("space", None))
    out_specs = (P("space", None), P("space", None))
    S, Q = mesh.shape["space"], mesh.shape["kern"]
    whole_tiles = Q == 4 and S % Q == 0 and (B // S // Q) % 16 == 0 and (G // S) % 128 == 0
    body = functools.partial(fast, S, Q) if whole_tiles else local
    return jax.shard_map(body, mesh=mesh, in_specs=in_specs, out_specs=out_specs, check_vma=False)
```
